32 devices in a mesh: seq: 16 (over z, y, core), mp: 2 (over x).
Axes of the slice: x: 2, y: 2, z: 4, core: 2. Of those that a mesh axis runs over, the one named last changes fastest.
Arguments:
- tokens: bfloat16 [6144, 3072], P('seq', 'mp'), may hold values from -6 to 6
- w_qkv: bfloat16 [3072, 3, 3072], P(None, None, 'mp'), may hold values from -1 to 1
- q_gain: float32 [128], replicated, may hold values from 0 to 5
- k_gain: float32 [128], replicated, may hold values from 0 to 5
- w_out: bfloat16 [3072, 3072], P('mp'), may hold values from -0.15625 to 0.15625
- neighbours: int32 [16, 6], replicated, may hold values from 0 to 15, as said below
- counts: int32 [16], replicated, may hold values from 1 to 6
Outputs:
- mixed: bfloat16 [6144, 3072], P('seq', 'mp')
The draws below stay inside these ranges and needn't reach their ends.
Inputs may be any that keep to these rules, and one draw needn't show every extreme that they name: `neighbours`: each row lists distinct tiles, each within 4 tiles of the row's own tile counted cyclically modulo 16.
All inputs are finite; a program needn't handle non-finite values.
Results may differ from the reference program's by a relative error of at most 0.014.
Values may be sent and summed in bfloat16 or wider, within the bound.
A program may use at most 192 MiB of HBM per device.

```python
import math
import jax
import jax.numpy as jnp
from jax import lax

D = 3072
HEADS = 24
HD = 128
TILE = 384
REACH = 4
NB = 6
TILES = 16
TOKENS = 6144
H_DEV = 12


def draw_w_qkv(key, part):
    first_key = jax.random.fold_in(jax.random.fold_in(key, 11), 0)
    base = jax.random.truncated_normal(first_key, -5.0, 5.0, (D, 3, HEADS * HD), jnp.float32) / math.sqrt(D)
    return base.astype(jnp.bfloat16)


def gain_draw(key, salt):
    inner = jax.random.fold_in(key, salt)
    return jnp.exp(jax.random.uniform(inner, (HD,), jnp.float32, math.log(0.6), math.log(1.6)))


def draw_q_gain(key, part):
    return gain_draw(key, 21)


def draw_k_gain(key, part):
    return gain_draw(key, 22)


def draw_neighbours(key, part):
    breadth = 2 * REACH + 1
    ranking = jax.random.randint(jax.random.fold_in(key, 31), (TILES, breadth), 0, 1 << 20) * 32 + jnp.arange(breadth, dtype=jnp.int32)
    picked = jnp.argsort(ranking, axis=1)[:, :NB].astype(jnp.int32) - REACH
    pinned = [-REACH, REACH, -1, 1] + [value for value in range(-REACH + 1, REACH) if value not in (-1, 0, 1)] + [0]
    picked = picked.at[0].set(jnp.array(pinned[:NB], dtype=jnp.int32))
    return ((jnp.arange(TILES, dtype=jnp.int32)[:, None] + picked) % TILES).astype(jnp.int32)


def draw_counts(key, part):
    drawn = jax.random.randint(jax.random.fold_in(key, 41), (TILES,), 1, NB + 1).astype(jnp.int32)
    return drawn.at[0].set(NB).at[1].set(1)


def spiked(entries, rng, source, target, parts, factor):
    def block_of(dim):
        return (jnp.arange(entries.shape[dim]) // (entries.shape[dim] // parts)).reshape((-1,) + (1,) * (entries.ndim - 1 - dim))

    near = jax.random.permutation(rng, parts)[block_of(target)]
    second = (block_of(target) + parts // 2) % parts
    return jnp.where((block_of(source) == near) | (block_of(source) == second), factor * entries, entries)


def shard_levels(rng, dims, cuts, least, top_value):
    gain = 1.0
    for position, shards_of in cuts:
        draws = jax.random.uniform(jax.random.fold_in(jax.random.fold_in(rng, 6), position), (shards_of,), jnp.float32, least / len(cuts), top_value / len(cuts))
        gain = gain * jnp.repeat(jnp.exp(draws), dims[position] // shards_of).reshape((-1,) + (1,) * (len(dims) - 1 - position))
    return gain


def normal_values(stream_key, dims, spread, limit, shards=(), kind=jnp.bfloat16):
    entries = jax.random.normal(stream_key, dims, jnp.float32) * spread
    if len(shards) > 0:
        entries = shard_levels(stream_key, dims, shards, -0.22, 0.18) * entries
    return jnp.clip(entries, min=-limit, max=limit).astype(kind)


def bell_draw_with(stream_key, dims, deviation, reach, pieces, heavy, kind=jnp.bfloat16):
    values = deviation * jax.random.normal(stream_key, dims, jnp.float32)
    if pieces:
        values = values * shard_levels(stream_key, dims, pieces, -0.22, 0.18)
    return jnp.clip(spiked(values, jax.random.fold_in(stream_key, 3), *heavy), -reach, reach).astype(kind)


def setup_inputs(seed: int = 0) -> dict:
    keys = jax.random.split(jax.random.key(seed), 8)
    tokens = normal_values(keys[0], (TOKENS, D), 1.0, 6.0, ((0, 16), (1, 2)))
    w_qkv = draw_w_qkv(jax.random.fold_in(keys[7], 71), 0)
    q_gain = draw_q_gain(jax.random.fold_in(keys[7], 71), 0)
    k_gain = draw_k_gain(jax.random.fold_in(keys[7], 71), 0)
    w_out = bell_draw_with(keys[4], (HEADS * HD, D), (HEADS * HD) ** -0.5, 0.15625, ((0, 2),), (0, 1, 2, 2.0))
    neighbours = draw_neighbours(jax.random.fold_in(keys[7], 71), 0)
    counts = draw_counts(jax.random.fold_in(keys[7], 71), 0)
    return {"tokens": tokens, "w_qkv": w_qkv, "q_gain": q_gain, "k_gain": k_gain, "w_out": w_out, "neighbours": neighbours, "counts": counts}


def head_norm(projected, gain_vec):
    per_head = projected.reshape(projected.shape[0], HEADS, HD)
    factor = lax.rsqrt(lax.optimization_barrier(jnp.mean(per_head * per_head, axis=-1, keepdims=True)) + 1e-06)
    return (per_head * factor * gain_vec).astype(jnp.bfloat16)

def reference(tokens, w_qkv, q_gain, k_gain, w_out, neighbours, counts):
    queries = head_norm(jnp.dot(tokens, w_qkv[:, 0, :], preferred_element_type=jnp.float32), q_gain)
    key_rows = head_norm(jnp.dot(tokens, w_qkv[:, 1, :], preferred_element_type=jnp.float32), k_gain)
    value_rows = jnp.dot(tokens, w_qkv[:, 2, :], preferred_element_type=jnp.float32).astype(jnp.bfloat16)
    queries = lax.optimization_barrier(queries)
    key_rows = lax.optimization_barrier(key_rows)
    value_rows = lax.optimization_barrier(value_rows)
    query_tiles = queries.reshape(TILES, TILE, HEADS, HD)
    key_tiles = key_rows.reshape(TILES, TILE, HEADS, HD)
    value_tiles = value_rows.reshape(TILES, TILE, HEADS, HD)
    factor = HD ** (-0.5)

    def one_tile(index):
        query_block = query_tiles[index].astype(jnp.float32)
        listed = neighbours[index]
        near_keys = key_tiles[listed].reshape(NB * TILE, HEADS, HD).astype(jnp.float32)
        near_values = value_tiles[listed].reshape(NB * TILE, HEADS, HD).astype(jnp.float32)
        usable = jnp.repeat(jnp.arange(NB, dtype=jnp.int32) < counts[index], TILE)
        scores = jnp.einsum('qhd,khd->hqk', query_block, near_keys) * factor
        scores = jnp.where(usable[None, None, :], scores, -jnp.inf)
        highest = lax.optimization_barrier(jnp.max(scores, axis=-1, keepdims=True))
        expo = jnp.exp(scores - highest)
        probs = (expo / lax.optimization_barrier(jnp.sum(expo, axis=-1, keepdims=True))).astype(jnp.bfloat16)
        probs = lax.optimization_barrier(probs)
        result = jnp.einsum('hqk,khd->qhd', probs.astype(jnp.float32), near_values)
        return result.astype(jnp.bfloat16)
    attended = lax.map(one_tile, jnp.arange(TILES, dtype=jnp.int32)).reshape(TOKENS, HEADS * HD)
    summed = jnp.zeros((TOKENS, D), jnp.float32)
    group_cols = H_DEV * HD
    for group in range(HEADS // H_DEV):
        lower = group * group_cols
        term = jnp.dot(attended[:, lower:lower + group_cols], w_out[lower:lower + group_cols], preferred_element_type=jnp.float32).astype(jnp.bfloat16)
        term = lax.optimization_barrier(term)
        summed = summed + term.astype(jnp.float32)
    return summed.astype(jnp.bfloat16)
```

```python
import functools

import jax
import jax.numpy as jnp
from jax import lax
from jax.experimental import pallas as pl
from jax.experimental.pallas import tpu as pltpu
from jax.sharding import PartitionSpec as P

HD = 128
TILE = 384
EPS = 1e-06
LOG2E = 1.4426950408889634
VMEM = 48 * 1024 * 1024


def width_of(columns):
    return 256 if columns % 256 == 0 else 128


def normed(product, gain):
    parts = []
    for first in range(0, product.shape[1], HD):
        head = product[:, first : first + HD]
        factor = lax.rsqrt(jnp.mean(head * head, axis=-1, keepdims=True) + EPS)
        parts.append(head * factor * gain)
    return parts[0] if len(parts) == 1 else jnp.concatenate(parts, axis=1)


def project_kernel(low_ref, high_ref, w_ref, gain_ref, out_ref):
    half = low_ref.shape[1]
    product = jnp.dot(low_ref[...], w_ref[0, :half, :], preferred_element_type=jnp.float32)
    product += jnp.dot(high_ref[...], w_ref[0, half:, :], preferred_element_type=jnp.float32)

    @pl.when(pl.program_id(0) == 0)
    def _():
        out_ref[0] = normed(product, gain_ref[...]).astype(out_ref.dtype)

    @pl.when(pl.program_id(0) != 0)
    def _():
        out_ref[0] = product.astype(out_ref.dtype)


def project(low, high, w, gain, kind, kinds, first_col, columns):
    rows, half = low.shape
    depth = w.shape[1]
    wide = width_of(columns)
    base = first_col // wide
    return pl.pallas_call(
        project_kernel,
        grid=(kinds, columns // wide),
        in_specs=[
            pl.BlockSpec((rows, half), lambda i, j: (0, 0)),
            pl.BlockSpec((rows, half), lambda i, j: (0, 0)),
            pl.BlockSpec((1, depth, wide), lambda i, j: (kind + i, 0, base + j)),
            pl.BlockSpec((1, HD), lambda i, j: (0, 0)),
        ],
        out_specs=pl.BlockSpec((1, rows, wide), lambda i, j: (i, 0, j)),
        out_shape=jax.ShapeDtypeStruct((kinds, rows, columns), jnp.bfloat16),
        compiler_params=pltpu.CompilerParams(vmem_limit_bytes=VMEM),
        cost_estimate=pl.CostEstimate(
            flops=2 * rows * depth * columns * kinds,
            bytes_accessed=2 * depth * columns * kinds + 2 * rows * (depth + columns * kinds),
            transcendentals=0,
        ),
        name="project",
    )(low, high, w, gain)


def attend_kernel(used_ref, q_ref, *refs):
    blocks = refs[:9]
    out_ref, top, total, acc = refs[9:]
    top[...] = jnp.full(top.shape, -jnp.inf, jnp.float32)
    total[...] = jnp.zeros(total.shape, jnp.float32)
    acc[...] = jnp.zeros(acc.shape, jnp.float32)
    scale = HD ** (-0.5) * LOG2E
    for index, block in enumerate(blocks):

        @pl.when(used_ref[index] != 0)
        def _(block=block):
            scores = lax.dot_general(
                block[0], q_ref[0], (((1,), (1,)), ((), ())), preferred_element_type=jnp.float32
            ) * scale
            before = top[...]
            now = jnp.maximum(before, jnp.max(scores, axis=0, keepdims=True))
            shrink = jnp.exp2(before - now)
            expo = jnp.exp2(scores - now)
            top[...] = now
            total[...] = total[...] * shrink + jnp.sum(expo, axis=0, keepdims=True)
            acc[...] = acc[...] * shrink + lax.dot_general(
                block[1],
                expo.astype(jnp.bfloat16),
                (((0,), (0,)), ((), ())),
                preferred_element_type=jnp.float32,
            )

    out_ref[...] = (acc[...] / total[...]).T.astype(out_ref.dtype)


def attend(used, queries, blocks, first_col, columns):
    rows = queries.shape[1]
    base = first_col // HD
    heads = columns // HD
    pair = pl.BlockSpec((2, rows, HD), lambda h, used: (0, 0, h))
    return pl.pallas_call(
        attend_kernel,
        grid_spec=pltpu.PrefetchScalarGridSpec(
            num_scalar_prefetch=1,
            grid=(heads,),
            in_specs=[pl.BlockSpec((1, rows, HD), lambda h, used: (0, 0, base + h))] + [pair] * 9,
            out_specs=pl.BlockSpec((rows, HD), lambda h, used: (0, h)),
            scratch_shapes=[
                pltpu.VMEM((1, rows), jnp.float32),
                pltpu.VMEM((1, rows), jnp.float32),
                pltpu.VMEM((HD, rows), jnp.float32),
            ],
        ),
        out_shape=jax.ShapeDtypeStruct((rows, columns), jnp.bfloat16),
        compiler_params=pltpu.CompilerParams(vmem_limit_bytes=VMEM),
        cost_estimate=pl.CostEstimate(
            flops=4 * rows * rows * 9 * columns,
            bytes_accessed=2 * rows * columns * 20,
            transcendentals=9 * rows * rows * heads,
        ),
        name="attend",
    )(used, queries, *blocks)


def mix_kernel(chunks, side_ref, *refs):
    own, other = refs[:chunks], refs[chunks : 2 * chunks]
    w_own, w_low, w_high, out_ref = refs[2 * chunks :]
    columns = own[0].shape[1]
    half = w_low.shape[0]
    product = jnp.zeros(out_ref.shape, jnp.float32)
    mine = jnp.concatenate([piece[...] for piece in own], axis=1)
    theirs = jnp.concatenate([piece[...] for piece in other], axis=1)
    product = jnp.dot(mine, w_own[...], preferred_element_type=jnp.float32)
    product += jnp.dot(theirs[:, :half], w_low[...], preferred_element_type=jnp.float32)
    product += jnp.dot(theirs[:, half:], w_high[...], preferred_element_type=jnp.float32)
    out_ref[...] = product.astype(out_ref.dtype)


def mix(side, own, other, w_out, w_low, w_high):
    rows, columns = own[0].shape
    depth = w_out.shape[0]
    width = w_low.shape[1]
    wide = width_of(width)
    steps = width // wide
    piece = pl.BlockSpec((rows, columns), lambda j, side: (0, 0))
    half = pl.BlockSpec((depth // 2, wide), lambda j, side: (0, j))
    return pl.pallas_call(
        functools.partial(mix_kernel, len(own)),
        grid_spec=pltpu.PrefetchScalarGridSpec(
            num_scalar_prefetch=1,
            grid=(steps,),
            in_specs=[piece] * (2 * len(own))
            + [pl.BlockSpec((depth, wide), lambda j, side: (0, side[0] * steps + j)), half, half],
            out_specs=pl.BlockSpec((rows, wide), lambda j, side: (0, j)),
        ),
        out_shape=jax.ShapeDtypeStruct((rows, width), jnp.bfloat16),
        compiler_params=pltpu.CompilerParams(vmem_limit_bytes=VMEM),
        cost_estimate=pl.CostEstimate(
            flops=4 * rows * depth * width, bytes_accessed=4 * depth * width, transcendentals=0
        ),
        name="mix",
    )(side, *own, *other, w_out, w_low, w_high)


def shifted(value, axis, target):
    count = lax.axis_size(axis)
    return lax.ppermute(value, axis, [(s, target(s) % count) for s in range(count)])


def on_device(tokens, w_qkv, q_gain, k_gain, w_out, neighbours, counts):
    columns = w_qkv.shape[2]
    heads_here = columns // HD
    total_tiles = neighbours.shape[0]
    sides = lax.axis_size("mp")
    side = lax.axis_index("mp")
    tile = lax.axis_index("seq")
    core, row = tile % 2, (tile // 2) % 2
    parts = 3 if heads_here % 3 == 0 else 1
    part_cols = columns // parts

    w = jnp.transpose(w_qkv, (1, 0, 2))
    q_gain, k_gain = q_gain.reshape(1, HD), k_gain.reshape(1, HD)

    if sides == 2:
        across = shifted(tokens, "mp", lambda s: s + 1)
        low = jnp.where(side == 0, tokens, across)
        high = jnp.where(side == 0, across, tokens)
    else:
        across = lax.all_gather(tokens, "mp", axis=1, tiled=True)
        low, high = jnp.split(across, 2, axis=1)

    turn = jnp.where(row == 0, -4, 4)
    spin = jnp.where(core == 0, -4, 4)
    held = jnp.stack(
        [tile, tile - 4, tile + 4, tile ^ 2, (tile ^ 2) + turn,
         tile ^ 1, (tile ^ 1) + spin, tile ^ 3, (tile ^ 3) + turn]
    )
    held = jnp.mod(held, total_tiles)
    listed = lax.dynamic_index_in_dim(neighbours, tile, 0, keepdims=False)
    in_use = jnp.arange(listed.shape[0], dtype=jnp.int32) < counts[tile]
    used = jnp.any((held[:, None] == listed[None, :]) & in_use[None, :], axis=1).astype(jnp.int32)

    windows = []
    for part in range(parts):
        own = project(low, high, w, k_gain, 1, 2, part * part_cols, part_cols)
        below = shifted(own, "seq", lambda s: s + 4)
        above = shifted(own, "seq", lambda s: s - 4)
        beside = shifted(own, "seq", lambda s: s ^ 2)
        twin = shifted(own, "seq", lambda s: s ^ 1)
        beyond = shifted(jnp.where(row == 1, below, above), "seq", lambda s: s ^ 2)
        twin_far = shifted(jnp.where(core == 1, below, above), "seq", lambda s: s ^ 1)
        twin_beside = shifted(beside, "seq", lambda s: s ^ 1)
        twin_beyond = shifted(beyond, "seq", lambda s: s ^ 1)
        windows.append(
            [own, below, above, beside, beyond, twin, twin_far, twin_beside, twin_beyond]
        )
    queries = project(low, high, w, q_gain, 0, 1, 0, columns)

    if sides == 2:
        depth, width = w_out.shape[0] // 2, w_out.shape[1] // 2
        sent = lax.dynamic_slice(w_out, (core * depth, (1 - side) * width), (depth, width))
        sent, _ = lax.optimization_barrier((sent, across))
        got = shifted(sent, "mp", lambda s: s + 1)
        got_twin = shifted(got, "seq", lambda s: s ^ 1)
        w_low = jnp.where(core == 0, got, got_twin)
        w_high = jnp.where(core == 0, got_twin, got)

    attended = [
        attend(used, queries, windows[part], part * part_cols, part_cols) for part in range(parts)
    ]
    if sides == 2:
        other = [shifted(piece, "mp", lambda s: s + 1) for piece in attended]
        return mix(side.reshape(1).astype(jnp.int32), attended, other, w_out, w_low, w_high)
    terms = jnp.dot(
        jnp.concatenate(attended, axis=1), w_out, preferred_element_type=jnp.float32
    ).astype(jnp.bfloat16)
    return lax.psum_scatter(terms, "mp", scatter_dimension=1, tiled=True)


def solution(mesh):
    return jax.shard_map(
        on_device,
        mesh=mesh,
        in_specs=(P("seq", "mp"), P(None, None, "mp"), P(), P(), P("mp", None), P(), P()),
        out_specs=P("seq", "mp"),
        check_vma=False,
    )
```

```python
import functools

import jax
import jax.numpy as jnp
from jax import lax
from jax.experimental import pallas as pl
from jax.experimental.pallas import tpu as pltpu
from jax.sharding import PartitionSpec as P

HD = 128
TILE = 384
EPS = 1e-06
LOG2E = 1.4426950408889634
VMEM = 48 * 1024 * 1024


def width_of(columns):
    return 256 if columns % 256 == 0 else 128


def normed(product, gain):
    parts = []
    for first in range(0, product.shape[1], HD):
        head = product[:, first : first + HD]
        factor = lax.rsqrt(jnp.mean(head * head, axis=-1, keepdims=True) + EPS)
        parts.append(head * factor * gain)
    return parts[0] if len(parts) == 1 else jnp.concatenate(parts, axis=1)


def project_kernel(low_ref, high_ref, w_ref, gain_ref, out_ref):
    half = low_ref.shape[1]
    product = jnp.dot(low_ref[...], w_ref[0, :half, :], preferred_element_type=jnp.float32)
    product += jnp.dot(high_ref[...], w_ref[0, half:, :], preferred_element_type=jnp.float32)

    @pl.when(pl.program_id(0) == 0)
    def _():
        out_ref[0] = normed(product, gain_ref[...]).astype(out_ref.dtype)

    @pl.when(pl.program_id(0) != 0)
    def _():
        out_ref[0] = product.astype(out_ref.dtype)


def project(low, high, w, gain, kind, kinds, first_col, columns):
    rows, half = low.shape
    depth = w.shape[1]
    wide = width_of(columns)
    base = first_col // wide
    return pl.pallas_call(
        project_kernel,
        grid=(kinds, columns // wide),
        in_specs=[
            pl.BlockSpec((rows, half), lambda i, j: (0, 0)),
            pl.BlockSpec((rows, half), lambda i, j: (0, 0)),
            pl.BlockSpec((1, depth, wide), lambda i, j: (kind + i, 0, base + j)),
            pl.BlockSpec((1, HD), lambda i, j: (0, 0)),
        ],
        out_specs=pl.BlockSpec((1, rows, wide), lambda i, j: (i, 0, j)),
        out_shape=jax.ShapeDtypeStruct((kinds, rows, columns), jnp.bfloat16),
        compiler_params=pltpu.CompilerParams(vmem_limit_bytes=VMEM),
        cost_estimate=pl.CostEstimate(
            flops=2 * rows * depth * columns * kinds,
            bytes_accessed=2 * depth * columns * kinds + 2 * rows * (depth + columns * kinds),
            transcendentals=0,
        ),
        name="project",
    )(low, high, w, gain)


def attend_kernel(pieces, used_ref, q_ref, *refs):
    blocks = [refs[first : first + pieces] for first in range(0, 9 * pieces, pieces)]
    out_ref, top, total, acc = refs[9 * pieces :]
    top[...] = jnp.full(top.shape, -jnp.inf, jnp.float32)
    total[...] = jnp.zeros(total.shape, jnp.float32)
    acc[...] = jnp.zeros(acc.shape, jnp.float32)
    scale = HD ** (-0.5) * LOG2E
    heads = q_ref.shape[2] // HD
    for index, block in enumerate(blocks):

        @pl.when(used_ref[index] != 0)
        def _(block=block):
            for piece in block:
                for head in range(heads):
                    cols = slice(head * HD, (head + 1) * HD)
                    scores = lax.dot_general(
                        piece[0, :, cols],
                        q_ref[0, :, cols],
                        (((1,), (1,)), ((), ())),
                        preferred_element_type=jnp.float32,
                    ) * scale
                    before = top[head]
                    now = jnp.maximum(before, jnp.max(scores, axis=0, keepdims=True))
                    shrink = jnp.exp2(before - now)
                    expo = jnp.exp2(scores - now)
                    top[head] = now
                    total[head] = total[head] * shrink + jnp.sum(expo, axis=0, keepdims=True)
                    acc[head] = acc[head] * shrink + lax.dot_general(
                        piece[1, :, cols],
                        expo.astype(jnp.bfloat16),
                        (((0,), (0,)), ((), ())),
                        preferred_element_type=jnp.float32,
                    )

    for head in range(heads):
        cols = slice(head * HD, (head + 1) * HD)
        out_ref[:, cols] = (acc[head] / total[head]).T.astype(out_ref.dtype)


def attend(used, queries, blocks, first_col, columns):
    rows = queries.shape[1]
    wide = width_of(columns)
    base = first_col // wide
    heads = wide // HD
    pieces = len(blocks[0])
    flat = [piece for block in blocks for piece in block]
    specs = [pl.BlockSpec((2, piece.shape[1], wide), lambda h, used: (0, 0, h)) for piece in flat]
    return pl.pallas_call(
        functools.partial(attend_kernel, pieces),
        grid_spec=pltpu.PrefetchScalarGridSpec(
            num_scalar_prefetch=1,
            grid=(columns // wide,),
            in_specs=[pl.BlockSpec((1, rows, wide), lambda h, used: (0, 0, base + h))] + specs,
            out_specs=pl.BlockSpec((rows, wide), lambda h, used: (0, h)),
            scratch_shapes=[
                pltpu.VMEM((heads, 1, rows), jnp.float32),
                pltpu.VMEM((heads, 1, rows), jnp.float32),
                pltpu.VMEM((heads, HD, rows), jnp.float32),
            ],
        ),
        out_shape=jax.ShapeDtypeStruct((rows, columns), jnp.bfloat16),
        compiler_params=pltpu.CompilerParams(vmem_limit_bytes=VMEM),
        cost_estimate=pl.CostEstimate(
            flops=24 * rows * rows * 9 * columns,
            bytes_accessed=2 * rows * columns * 20,
            transcendentals=9 * rows * rows * (columns // HD),
        ),
        name="attend",
    )(used, queries, *flat)


def mix_kernel(first, side_ref, own_ref, other_ref, w_own, w_other, *refs):
    out_ref = refs[-1]
    product = jnp.dot(own_ref[...], w_own[...], preferred_element_type=jnp.float32)
    product += jnp.dot(other_ref[...], w_other[...], preferred_element_type=jnp.float32)
    if not first:
        product += refs[0][...]
    out_ref[...] = product.astype(out_ref.dtype)


def mix(side, own, other, w_out, w_other, first_col, so_far, kind):
    rows, columns = own.shape
    width = w_other.shape[1]
    wide = width_of(width)
    steps = width // wide
    base = first_col // columns
    piece = pl.BlockSpec((rows, columns), lambda j, side: (0, 0))
    strip = pl.BlockSpec((rows, wide), lambda j, side: (0, j))
    more = [] if so_far is None else [so_far]
    return pl.pallas_call(
        functools.partial(mix_kernel, so_far is None),
        grid_spec=pltpu.PrefetchScalarGridSpec(
            num_scalar_prefetch=1,
            grid=(steps,),
            in_specs=[
                piece,
                piece,
                pl.BlockSpec((columns, wide), lambda j, side: (base, side[0] * steps + j)),
                pl.BlockSpec((columns, wide), lambda j, side: (base, j)),
            ]
            + [strip] * len(more),
            out_specs=strip,
        ),
        out_shape=jax.ShapeDtypeStruct((rows, width), kind),
        compiler_params=pltpu.CompilerParams(vmem_limit_bytes=VMEM),
        cost_estimate=pl.CostEstimate(
            flops=4 * rows * columns * width, bytes_accessed=4 * columns * width, transcendentals=0
        ),
        name="mix",
    )(side, own, other, w_out, w_other, *more)


def after(value, *others):
    return lax.optimization_barrier((value,) + others)[0]


def shifted(value, axis, target):
    count = lax.axis_size(axis)
    return lax.ppermute(value, axis, [(s, target(s) % count) for s in range(count)])


def on_device(tokens, w_qkv, q_gain, k_gain, w_out, neighbours, counts):
    columns = w_qkv.shape[2]
    heads_here = columns // HD
    total_tiles = neighbours.shape[0]
    sides = lax.axis_size("mp")
    side = lax.axis_index("mp")
    tile = lax.axis_index("seq")
    core, row = tile % 2, (tile // 2) % 2
    splits = (4, 4, 2, 2) if heads_here == 12 else (1,) * heads_here
    widths = [heads * HD for heads in splits]
    starts = [sum(widths[:part]) for part in range(len(widths))]

    w = jnp.transpose(w_qkv, (1, 0, 2))
    q_gain, k_gain = q_gain.reshape(1, HD), k_gain.reshape(1, HD)

    if sides == 2:
        mine = jnp.split(tokens, 2, axis=0)
        across = [shifted(half, "mp", lambda s: s + 1) for half in mine]
        lows = [jnp.where(side == 0, here, there) for here, there in zip(mine, across)]
        highs = [jnp.where(side == 0, there, here) for here, there in zip(mine, across)]
    else:
        across = [lax.all_gather(tokens, "mp", axis=1, tiled=True)]
        low, high = jnp.split(across[0], 2, axis=1)
        lows, highs = [low], [high]

    turn = jnp.where(row == 0, -4, 4)
    spin = jnp.where(core == 0, -4, 4)
    held = jnp.stack(
        [tile, tile - 4, tile + 4, tile ^ 2, (tile ^ 2) + turn,
         tile ^ 1, (tile ^ 1) + spin, tile ^ 3, (tile ^ 3) + turn]
    )
    held = jnp.mod(held, total_tiles)
    listed = lax.dynamic_index_in_dim(neighbours, tile, 0, keepdims=False)
    in_use = jnp.arange(listed.shape[0], dtype=jnp.int32) < counts[tile]
    used = jnp.any((held[:, None] == listed[None, :]) & in_use[None, :], axis=1).astype(jnp.int32)

    low = high = queries = None
    windows, attended = [], []
    past_beyond = None
    for part in range(len(widths)):
        start, width = starts[part], widths[part]
        if part == 0:
            owns = [project(a, b, w, k_gain, 1, 2, start, width) for a, b in zip(lows, highs)]
        else:
            if part == 1:
                low, high = jnp.concatenate(lows, axis=0), jnp.concatenate(highs, axis=0)
            if part == 2:
                low, high, _ = lax.optimization_barrier((low, high, queries))
            owns = [project(low, high, w, k_gain, 1, 2, start, width)]
        pieces = []
        for own in owns:
            below = shifted(own, "seq", lambda s: s + 4)
            above = shifted(own, "seq", lambda s: s - 4)
            held_up = own if past_beyond is None else after(own, past_beyond)
            beside = shifted(held_up, "seq", lambda s: s ^ 2)
            twin = shifted(own, "seq", lambda s: s ^ 1)
            onward = jnp.where(row == 1, below, above)
            if part >= 2:
                onward = after(onward, attended[part - 2])
            beyond = shifted(onward, "seq", lambda s: s ^ 2)
            past_beyond = beyond
            twin_far = shifted(jnp.where(core == 1, below, above), "seq", lambda s: s ^ 1)
            twin_beside = shifted(beside, "seq", lambda s: s ^ 1)
            handed = beyond if part < 2 else after(beyond, attended[part - 1])
            twin_beyond = shifted(handed, "seq", lambda s: s ^ 1)
            pieces.append(
                [own, below, above, beside, beyond, twin, twin_far, twin_beside, twin_beyond]
            )
        window = [list(block) for block in zip(*pieces)]
        windows.append(window)
        if part == 1:
            queries = project(low, high, w, q_gain, 0, 1, 0, columns)
        if part >= 1:
            for done in range(len(attended), part + 1):
                attended.append(attend(used, queries, windows[done], starts[done], widths[done]))

    if sides == 2:
        depth, width = w_out.shape[0] // 2, w_out.shape[1] // 2
        sent = lax.dynamic_slice(w_out, (core * depth, (1 - side) * width), (depth, width))
        sent = after(sent, *across)
        got = shifted(sent, "mp", lambda s: s + 1)
        got_twin = shifted(got, "seq", lambda s: s ^ 1)
        w_other = jnp.concatenate(
            [jnp.where(core == 0, got, got_twin), jnp.where(core == 0, got_twin, got)], axis=0
        )
        flag = side.reshape(1).astype(jnp.int32)
        total = None
        for part, piece in enumerate(attended):
            other = shifted(piece, "mp", lambda s: s + 1)
            kind = jnp.bfloat16 if part == len(attended) - 1 else jnp.float32
            total = mix(flag, piece, other, w_out, w_other, starts[part], total, kind)
        return total
    terms = jnp.dot(
        jnp.concatenate(attended, axis=1), w_out, preferred_element_type=jnp.float32
    ).astype(jnp.bfloat16)
    return lax.psum_scatter(terms, "mp", scatter_dimension=1, tiled=True)


def solution(mesh):
    return jax.shard_map(
        on_device,
        mesh=mesh,
        in_specs=(P("seq", "mp"), P(None, None, "mp"), P(), P(), P("mp", None), P(), P()),
        out_specs=P("seq", "mp"),
        check_vma=False,
    )
```
